256 devices in a mesh: mem: 8 (over x_lo, y), tile: 32 (over x_hi, z, core).
Axes of the slice: x: 4 (x_hi: 2, x_lo: 2; x = x_hi * 2 + x_lo), y: 4, z: 8, core: 2. Of those that a mesh axis runs over, the one named last changes fastest.
Arguments:
- members: float32 [80, 2, 524288], P('mem', None, 'tile'), may hold values from -6 to 6
- increment: float32 [2, 2097152], P(None, 'tile'), may hold values from -6 to 6
- fine_angles: float32 [2, 2097152], P(None, 'tile'), may hold values from -1.5 to 1.5
- coarse_angles: float32 [2, 524288], P(None, 'tile'), may hold values from -1.5 to 1.5
- remap_weights: bfloat16 [32, 128, 4, 256, 128], P('tile', 'mem'), may hold values from -0.1875 to 0.1875
- sources: int32 [32, 128, 4], P('tile', 'mem'), may hold values from 0 to 8191, as said below
- counts: int32 [32, 128], P('tile', 'mem'), may hold values from 2 to 4, as said below
Outputs:
- recentered: float32 [80, 2, 524288], P('mem', None, 'tile')
The draws below stay inside these ranges and needn't reach their ends.
Inputs may be any that keep to these rules, and one draw needn't show every extreme that they name: `sources`: for entry [s, l], with g = 128 s + l, slots 0 and 1 name fine blocks 2 g and 2 g + 1; each further even slot names block (2 g - r) mod 8192 and each further odd slot block (2 g + 1 + r + 4096) mod 8192, each with its own r from 1 to 256. `counts`: every column shard holds a coarse block that uses all 4 slots.
All inputs are finite; a program needn't handle non-finite values.
Results may differ from the reference program's by a relative error of at most 0.0017.
Values may be sent and summed in bfloat16 or wider, within the bound.
No kernel may reach another device: no remote copies, remote signals or barrier semaphores. Data moves between devices by JAX's collectives and lax.ppermute only.
A program may use at most 64 MiB of HBM per device.

```python
import jax
import jax.numpy as jnp
from jax import lax

BC = 128
BF = 256
KMAX = 4
MEMBERS = 80
CBT = 128
SHARDS = 32
NC = 524288
NFB = 8192
NF = 2097152


def draw_sources(key, part):
    numbers = jnp.arange(SHARDS * CBT, dtype=jnp.int32).reshape(SHARDS, CBT, 1)
    reach = jax.random.randint(jax.random.fold_in(key, 11), (SHARDS, CBT, KMAX - 2), 1, 2 * CBT + 1, dtype=jnp.int32)
    sides = jnp.arange(KMAX - 2, dtype=jnp.int32) % 2
    below = jnp.mod(2 * numbers - reach, NFB)
    across = jnp.mod(2 * numbers + 1 + reach + NFB // 2, NFB)
    others = jnp.where(sides[None, None, :] == 0, below, across).astype(jnp.int32)
    return jnp.concatenate([2 * numbers, 2 * numbers + 1, others], axis=2).astype(jnp.int32)


def draw_counts(key, part):
    drawn = jax.random.randint(jax.random.fold_in(key, 7), (SHARDS, CBT), 2, KMAX + 1, dtype=jnp.int32)
    full_at = jax.random.randint(jax.random.fold_in(key, 8), (SHARDS, 1), 0, CBT, dtype=jnp.int32)
    positions = jnp.arange(CBT, dtype=jnp.int32)[None, :]
    return jnp.where(positions == full_at, KMAX, drawn).astype(jnp.int32)


def block_levels(key, shape, pieces, least, high):
    gain = 1.0
    for axis_at, blocks in pieces:
        draws = jax.random.uniform(jax.random.fold_in(jax.random.fold_in(key, 6), axis_at), (blocks,), jnp.float32, least / len(pieces), high / len(pieces))
        gain = gain * jnp.repeat(jnp.exp(draws), shape[axis_at] // blocks).reshape((-1,) + (1,) * (len(shape) - 1 - axis_at))
    return gain


def noise(key, shape, spread, most, shards=(), held_as=jnp.bfloat16):
    array = spread * jax.random.normal(key, shape, jnp.float32)
    if shards:
        array = array * block_levels(key, shape, shards, -0.22, 0.18)
    return jnp.clip(array, -most, most).astype(held_as)


def setup_inputs(seed: int = 0) -> dict:
    arg_keys = jax.random.split(jax.random.key(seed), 8)
    return {
        "members": noise(arg_keys[0], (MEMBERS, 2, NC), 1.0, 6.0, ((0, 8), (2, 32)), jnp.float32),
        "increment": noise(arg_keys[1], (2, NF), 1.0, 6.0, ((1, 32),), jnp.float32),
        "fine_angles": jnp.clip(jax.random.uniform(arg_keys[2], (2, NF), jnp.float32, -1.5, 1.5) * block_levels(arg_keys[2], (2, NF), ((1, 32),), -0.4, 0.0), -1.5, 1.5),
        "coarse_angles": jnp.clip(jax.random.uniform(arg_keys[3], (2, NC), jnp.float32, -1.5, 1.5) * block_levels(arg_keys[3], (2, NC), ((1, 32),), -0.4, 0.0), -1.5, 1.5),
        "remap_weights": noise(arg_keys[4], (SHARDS, CBT, KMAX, BF, BC), (KMAX * BF) ** -0.5, 0.1875, ((0, 32), (1, 8))),
        "sources": draw_sources(jax.random.fold_in(arg_keys[7], 71), 0),
        "counts": draw_counts(jax.random.fold_in(arg_keys[7], 71), 0),
    }


def to_vector(east_part, north_part, longitude, latitude):
    sin_lon, cos_lon = jnp.sin(longitude), jnp.cos(longitude)
    sin_lat, cos_lat = jnp.sin(latitude), jnp.cos(latitude)
    first = -sin_lon * east_part - sin_lat * cos_lon * north_part
    second = cos_lon * east_part - sin_lat * sin_lon * north_part
    third = cos_lat * north_part
    return first, second, third


def to_wind(first, second, third, longitude, latitude):
    sin_lon, cos_lon = jnp.sin(longitude), jnp.cos(longitude)
    sin_lat, cos_lat = jnp.sin(latitude), jnp.cos(latitude)
    east_part = -sin_lon * first + cos_lon * second
    north_part = -sin_lat * cos_lon * first - sin_lat * sin_lon * second + cos_lat * third
    return jnp.stack([east_part, north_part])


def reference(members, increment, fine_angles, coarse_angles, remap_weights, sources, counts):
    first, second, third = to_vector(increment[0], increment[1], fine_angles[0], fine_angles[1])
    fine_cart = jnp.stack([first, second, third]).astype(jnp.bfloat16)
    blocks = fine_cart.reshape(3, NFB, BF).transpose(1, 0, 2)

    def one_shard(shard_data):
        shard_weights, source_ids, slot_counts = shard_data
        picked = blocks[source_ids]
        live_slots = jnp.arange(KMAX, dtype=jnp.int32)[None, :] < slot_counts[:, None]
        picked = jnp.where(live_slots[:, :, None, None], picked, 0)
        return jnp.einsum('ikcf,ikfb->cib', picked.astype(jnp.float32), shard_weights.astype(jnp.float32))

    coarse = lax.map(one_shard, (remap_weights, sources, counts))
    coarse_cart = coarse.transpose(1, 0, 2, 3).reshape(3, NC)
    coarse_wind = to_wind(coarse_cart[0], coarse_cart[1], coarse_cart[2], coarse_angles[0], coarse_angles[1])
    member_mean = jnp.sum(members, axis=0) / MEMBERS
    return members - member_mean[None] + coarse_wind[None]
```

```python
import jax
import jax.numpy as jnp
from jax import lax
from jax.experimental import pallas as pl
from jax.experimental.pallas import tpu as pltpu
from jax.sharding import PartitionSpec as P

F32 = jnp.float32
BF16 = jnp.bfloat16
VMEM = pl.BlockSpec(memory_space=pltpu.VMEM)
SMEM = pl.BlockSpec(memory_space=pltpu.SMEM)
ANY = pl.BlockSpec(memory_space=pl.ANY)


def sin_cos(x):
    y = x * x
    s = F32(1.0 / 6227020800.0)
    for c in (-1.0 / 39916800.0, 1.0 / 362880.0, -1.0 / 5040.0, 1.0 / 120.0, -1.0 / 6.0):
        s = s * y + F32(c)
    c_ = F32(1.0 / 479001600.0)
    for c in (-1.0 / 3628800.0, 1.0 / 40320.0, -1.0 / 720.0, 1.0 / 24.0, -0.5):
        c_ = c_ * y + F32(c)
    return x + x * (y * s), F32(1.0) + y * c_


def flat(x):
    lead, columns = x.shape[:-2], x.shape[-1]
    chunks = columns // 128
    x = x.reshape(*lead, 2, chunks, 128)
    return jnp.swapaxes(x, -3, -2).reshape(*lead, 2 * chunks, 128)


def unflat(x):
    lead, rows = x.shape[:-2], x.shape[-2]
    x = x.reshape(*lead, rows // 2, 2, 128)
    return jnp.swapaxes(x, -3, -2).reshape(*lead, 2, rows * 64)


def sum_kernel(half_ref, members_ref, mine_ref, other_ref):
    rows = mine_ref.shape[0]
    half = half_ref[0]
    mine_ref[...] = jnp.sum(members_ref[:, pl.ds(pl.multiple_of(half * rows, rows), rows), :], axis=0)
    other_ref[...] = jnp.sum(members_ref[:, pl.ds(pl.multiple_of((1 - half) * rows, rows), rows), :], axis=0)


def add_kernel(y_ref, mine_ref, got_ref, own_ref, *send_refs):
    rows = own_ref.shape[0]
    y = y_ref[0]
    for k, ref in enumerate((own_ref,) + send_refs):
        at = pl.ds(pl.multiple_of((y ^ k) * rows, rows), rows)
        ref[...] = mine_ref[at, :] + got_ref[at, :]


def cart_kernel(inc_ref, ang_ref, cart_ref):
    step = 64

    def body(n, carry):
        at = pl.ds(pl.multiple_of(n * step, step), step)
        s, c = sin_cos(ang_ref[at, :].reshape(step // 8, 8, 128))
        u = inc_ref[at, :].reshape(step // 8, 8, 128)
        su, cu = s * u, c * u
        t = pltpu.roll(su, 7, 1)
        cart_ref[0, at, :] = (-su - c * t).reshape(step, 128)
        cart_ref[1, at, :] = (cu - s * t).reshape(step, 128)
        cart_ref[2, at, :] = pltpu.roll(cu, 7, 1).reshape(step, 128)
        return carry

    lax.fori_loop(0, inc_ref.shape[0] // step, body, 0)


def gather_kernel(where_ref, own_ref, r17_ref, r16_ref, rup_ref, cart_ref,
                  s17_ref, s16_ref, sup_ref, near_ref, own2_ref, tmp_ref):
    m = where_ref[0]
    blocks = own_ref.shape[1]
    fine = cart_ref.shape[1] // 4
    for n, (ids, slot, out) in enumerate(
        ((r17_ref, 3, s17_ref), (r16_ref, 3, s16_ref), (rup_ref, 2, sup_ref), (own_ref, 2, own2_ref))
    ):
        for i in range(blocks):
            row = 4 * (ids[slot, i] & (fine - 1))
            for c in range(3):
                tmp_ref[n, 3 * i + c : 3 * i + c + 1, 0:128] = cart_ref[c, pl.ds(row, 1), :]
                tmp_ref[n, 3 * i + c : 3 * i + c + 1, 128:256] = cart_ref[c, pl.ds(row + 2, 1), :]
        out[...] = tmp_ref[n].astype(BF16)
    first = pl.multiple_of(m * (blocks * 8), 8)
    for k in range(2):
        for c in range(3):
            for h in range(2):
                near_ref[2 * k + h, pl.ds(c, blocks, stride=3), :] = (
                    cart_ref[c, pl.ds(first + 4 * k + 2 * h, blocks, stride=8), :]
                )


def near_kernel(near_ref, weights_ref, acc_ref, held, sems):
    blocks = weights_ref.shape[0]
    copies = [
        pltpu.make_async_copy(weights_ref.at[i, pl.ds(0, 2)], held.at[i], sems.at[i]) for i in range(blocks)
    ]
    for copy in copies:
        copy.start()
    for i in range(blocks):
        lhs = jnp.concatenate([near_ref[n, 3 * i : 3 * i + 3, :] for n in range(4)], axis=1).astype(BF16)
        copies[i].wait()
        acc_ref[3 * i : 3 * i + 3, :] = jnp.dot(
            lhs, held[i].reshape(512, 128), preferred_element_type=F32
        )


def far_kernel(where_ref, ids_ref, counts_ref, acc_ref, own2_ref, gup_ref, g16_ref, g17_ref, ang_ref,
               p0_ref, p1_ref, p2_ref, p3_ref, weights_ref, delta_ref, rows, cart, wind, held, sems):
    blocks = weights_ref.shape[0]
    tile, fine_bits, sixteen, members = where_ref[1], 8, where_ref[2], F32(80.0)
    copies = [
        pltpu.make_async_copy(weights_ref.at[i, pl.ds(2, 2)], held.at[i], sems.at[i]) for i in range(blocks)
    ]
    for copy in copies:
        copy.start()
    for n, ref in enumerate((own2_ref, gup_ref, g16_ref, g17_ref)):
        rows[n] = ref[...].astype(F32)
    for i in range(blocks):
        at = slice(3 * i, 3 * i + 3)
        count = counts_ref[0, i]
        two = jnp.where((ids_ref[2, i] >> fine_bits) == tile, rows[0, at, :], rows[1, at, :])
        three = jnp.where((ids_ref[3, i] >> fine_bits) == sixteen, rows[2, at, :], rows[3, at, :])
        two = jnp.where(count > 2, two, 0.0)
        three = jnp.where(count > 3, three, 0.0)
        lhs = jnp.concatenate([two, three], axis=1).astype(BF16)
        copies[i].wait()
        cart[at, :] = acc_ref[at, :] + jnp.dot(lhs, held[i].reshape(512, 128), preferred_element_type=F32)
    x, y, z = (cart[pl.ds(c, blocks, stride=3), :] for c in range(3))
    sa, ca = sin_cos(ang_ref[pl.ds(0, blocks, stride=2), :])
    sp, cp = sin_cos(ang_ref[pl.ds(1, blocks, stride=2), :])
    wind[pl.ds(0, blocks, stride=2), :] = -sa * x + ca * y
    wind[pl.ds(1, blocks, stride=2), :] = -sp * ca * x - sp * sa * y + cp * z
    mean = (p0_ref[...] + p1_ref[...] + p2_ref[...] + p3_ref[...]) / members
    delta = wind[...] - mean
    for n in range(delta_ref.shape[0]):
        delta_ref[n] = delta


def out_kernel(members_ref, delta_ref, out_ref):
    out_ref[...] = members_ref[...] + delta_ref[...][None]


def shards(members, increment, fine_angles, coarse_angles, remap_weights, sources, counts):
    mems, tiles = lax.axis_size("mem"), lax.axis_size("tile")
    m, t = lax.axis_index("mem"), lax.axis_index("tile")
    weights = remap_weights[0]
    blocks = weights.shape[0]
    ids = sources[0].T
    flip = mems // 2
    far = tiles // 2

    def send(x, mem_flip, tile_shift):
        pairs = [
            (a * tiles + b, (a ^ mem_flip) * tiles + (b + tile_shift) % tiles)
            for a in range(mems)
            for b in range(tiles)
        ]
        return lax.ppermute(x, ("mem", "tile"), pairs)

    where = jnp.stack([m, t, (t + far) % tiles, m // 4, m % 4]).astype(jnp.int32)
    r17 = send(ids, flip, far + 1)
    r16 = send(ids, flip, far)
    rup = send(ids, 0, -1)

    members_rows = flat(members)
    total_rows = members_rows.shape[1]
    half = total_rows // 2
    piece = total_rows // mems
    row = lambda n, dtype=F32: jax.ShapeDtypeStruct((n, 128), dtype)
    mine, other = pl.pallas_call(
        sum_kernel, out_shape=(row(half), row(half)), in_specs=[SMEM, VMEM], out_specs=(VMEM, VMEM), name="member_sum"
    )((m // 4).reshape(1), members_rows)
    got = send(other, flip, 0)

    inc_rows, ang_rows = flat(increment), flat(fine_angles)
    cart = pl.pallas_call(
        cart_kernel,
        out_shape=jax.ShapeDtypeStruct((3,) + inc_rows.shape, F32),
        in_specs=[VMEM, VMEM],
        out_specs=VMEM,
        name="fine_cart",
    )(inc_rows, ang_rows)

    rows = jax.ShapeDtypeStruct((3 * blocks, 256), BF16)
    s17, s16, sup, near, own2 = pl.pallas_call(
        gather_kernel,
        out_shape=(rows, rows, rows, jax.ShapeDtypeStruct((4, 3 * blocks, 128), F32), rows),
        in_specs=[SMEM] * 5 + [VMEM],
        out_specs=(VMEM,) * 5,
        scratch_shapes=[pltpu.VMEM((4, 3 * blocks, 256), F32)],
        name="pick_rows",
    )(where, ids, r17, r16, rup, cart)
    g17 = send(s17, flip, -(far + 1))
    g16 = send(s16, flip, -far)
    gup = send(sup, 0, 1)

    p0, q1, q2, q3 = pl.pallas_call(
        add_kernel, out_shape=(row(piece),) * 4, in_specs=[SMEM, VMEM, VMEM], out_specs=(VMEM,) * 4, name="pair_sum"
    )((m % 4).reshape(1), mine, got)
    p1, p2, p3 = send(q1, 1, 0), send(q2, 2, 0), send(q3, 3, 0)

    acc = pl.pallas_call(
        near_kernel,
        out_shape=row(3 * blocks),
        in_specs=[VMEM, ANY],
        out_specs=VMEM,
        scratch_shapes=[pltpu.VMEM((blocks, 2, 256, 128), BF16), pltpu.SemaphoreType.DMA((blocks,))],
        name="near_slots",
    )(near, weights)

    angles = lax.dynamic_slice_in_dim(flat(coarse_angles), m * piece, piece, 0)
    delta = pl.pallas_call(
        far_kernel,
        out_shape=jax.ShapeDtypeStruct((mems, piece, 128), F32),
        in_specs=[SMEM] * 3 + [VMEM] * 10 + [ANY],
        out_specs=VMEM,
        scratch_shapes=[
            pltpu.VMEM((4, 3 * blocks, 256), F32),
            pltpu.VMEM((3 * blocks, 128), F32),
            pltpu.VMEM((piece, 128), F32),
            pltpu.VMEM((blocks, 2, 256, 128), BF16),
            pltpu.SemaphoreType.DMA((blocks,)),
        ],
        name="far_slots",
    )(where, ids, counts, acc, own2, gup, g16, g17, angles, p0, p1, p2, p3, weights)
    whole = lax.all_to_all(delta, "mem", 0, 0, tiled=True).reshape(total_rows, 128)
    return unflat(members_rows + whole[None])


def solution(mesh):
    in_specs = (
        P("mem", None, "tile"),
        P(None, "tile"),
        P(None, "tile"),
        P(None, "tile"),
        P("tile", "mem", None, None, None),
        P("tile", "mem", None),
        P("tile", "mem"),
    )
    out_specs = P("mem", None, "tile")
    return jax.shard_map(shards, mesh=mesh, in_specs=in_specs, out_specs=out_specs, check_vma=False)
```

```python
import jax
import jax.numpy as jnp
from jax import lax
from jax.experimental import pallas as pl
from jax.experimental.pallas import tpu as pltpu
from jax.sharding import PartitionSpec as P

F32 = jnp.float32
BF16 = jnp.bfloat16
VMEM = pl.BlockSpec(memory_space=pltpu.VMEM)
SMEM = pl.BlockSpec(memory_space=pltpu.SMEM)
ANY = pl.BlockSpec(memory_space=pl.ANY)
HBM = pl.BlockSpec(memory_space=pltpu.HBM)


def placed(x, spec):
    if spec is VMEM:
        return pltpu.with_memory_space_constraint(x, pltpu.VMEM)
    return pltpu.with_memory_space_constraint(x, pltpu.HBM) if spec is HBM else x


def split(index, count, rows):
    return pl.ds(pl.multiple_of(index * rows, rows), rows)


def sin_cos(x):
    y = x * x
    s = F32(1.0 / 6227020800.0)
    for c in (-1.0 / 39916800.0, 1.0 / 362880.0, -1.0 / 5040.0, 1.0 / 120.0, -1.0 / 6.0):
        s = s * y + F32(c)
    c_ = F32(1.0 / 479001600.0)
    for c in (-1.0 / 3628800.0, 1.0 / 40320.0, -1.0 / 720.0, 1.0 / 24.0, -0.5):
        c_ = c_ * y + F32(c)
    return x + x * (y * s), F32(1.0) + y * c_


def flat(x):
    lead, columns = x.shape[:-2], x.shape[-1]
    chunks = columns // 128
    x = x.reshape(*lead, 2, chunks, 128)
    return jnp.swapaxes(x, -3, -2).reshape(*lead, 2 * chunks, 128)


def unflat(x):
    lead, rows = x.shape[:-2], x.shape[-2]
    x = x.reshape(*lead, rows // 2, 2, 128)
    return jnp.swapaxes(x, -3, -2).reshape(*lead, 2, rows * 64)


def pair_kernel(mine_ref, got_ref, after_ref, keep_ref, send_ref):
    del after_ref
    rows = keep_ref.shape[0]
    half = lax.rem(lax.axis_index("mem"), 2)
    for ref, part in ((keep_ref, half), (send_ref, 1 - half)):
        at = split(part, 2, rows)
        ref[...] = mine_ref[at, :] + got_ref[at, :]


def cart_kernel(inc_hbm, ang_hbm, cart_ref, even_ref, inc, ang, sems):
    parts = sems.shape[0]
    step = inc.shape[0] // parts
    loads = [
        [pltpu.make_async_copy(src.at[split(n, parts, step)], dst.at[split(n, parts, step)], sems.at[n, k])
         for k, (src, dst) in enumerate(((inc_hbm, inc), (ang_hbm, ang)))]
        for n in range(parts)
    ]
    for pair in loads:
        for load in pair:
            load.start()
    for n in range(parts):
        for load in loads[n]:
            load.wait()

        def body(k, carry, n=n):
            rows = 64
            at = pl.ds(pl.multiple_of(n * step + k * rows, rows), rows)
            s, c = sin_cos(ang[at, :].reshape(rows // 8, 8, 128))
            u = inc[at, :].reshape(rows // 8, 8, 128)
            su, cu = s * u, c * u
            t = pltpu.roll(su, 7, 1)
            cart_ref[0, at, :] = (-su - c * t).reshape(rows, 128)
            cart_ref[1, at, :] = (cu - s * t).reshape(rows, 128)
            cart_ref[2, at, :] = pltpu.roll(cu, 7, 1).reshape(rows, 128)
            return carry

        lax.fori_loop(0, step // 64, body, 0)
        half = step // 2
        for c in range(3):
            even_ref[c, n * half : (n + 1) * half, :] = cart_ref[c, pl.ds(n * step, half, stride=2), :].astype(BF16)


def sum_kernel(members_hbm, after_ref, members_ref, keep_ref, send_ref, sems):
    del after_ref
    count, rows = members_hbm.shape[0], keep_ref.shape[0]
    half = lax.axis_index("mem") // 4
    loads = [
        [pltpu.make_async_copy(members_hbm.at[n, split(h, 2, rows)], members_ref.at[n, split(h, 2, rows)], sems.at[n, k])
         for n in range(count)]
        for k, h in enumerate((1 - half, half))
    ]
    for part in loads:
        for load in part:
            load.start()
    for part, h, ref in ((loads[0], 1 - half, send_ref), (loads[1], half, keep_ref)):
        for load in part:
            load.wait()
        ref[...] = jnp.sum(members_ref[:, split(h, 2, rows), :], axis=0)


def pick_kernel(r17_ref, r16_ref, cart_ref, s17_ref, s16_ref, ids, tmp, sems):
    fine = cart_ref.shape[1] // 4
    asked = ((r17_ref, s17_ref), (r16_ref, s16_ref))
    copies = [pltpu.make_async_copy(ref, ids.at[n], sems.at[n]) for n, (ref, _) in enumerate(asked)]
    for copy in copies:
        copy.start()
    for copy in copies:
        copy.wait()
    for n, (ref, out) in enumerate(asked):
        for i in range(ref.shape[1]):
            row = 4 * (ids[n, 3, i] & (fine - 1))
            for c in range(3):
                for h in range(2):
                    tmp[n, 3 * i + c : 3 * i + c + 1, 128 * h : 128 * h + 128] = (
                        cart_ref[c, pl.ds(row + 2 * h, 1), :]
                    )
        out[...] = tmp[n].astype(BF16)


def near_kernel(ids_ref, counts_ref, cart_ref, below_ref, weights_ref, acc_ref, m16_ref, m17_ref, near, below):
    blocks = weights_ref.shape[0]
    fine = cart_ref.shape[1] // 4
    tiles = lax.axis_size("tile")
    tile = lax.axis_index("tile")
    across = lax.rem(tile + tiles // 2, tiles)
    first = pl.multiple_of(lax.axis_index("mem") * (blocks * 8), 8)
    below[...] = below_ref[...].astype(F32)
    for k in range(2):
        for c in range(3):
            for h in range(2):
                near[2 * k + h, pl.ds(c, blocks, stride=3), :] = (
                    cart_ref[c, pl.ds(first + 4 * k + 2 * h, blocks, stride=8), :]
                )
    for i in range(blocks):
        count, two, three = counts_ref[0, i], ids_ref[2, i], ids_ref[3, i]
        row, mine = two & (fine - 1), two // fine == tile
        for c in range(3):
            for h in range(2):
                got = jnp.where(mine, cart_ref[c, pl.ds(4 * row + 2 * h, 1), :], below[c, pl.ds(2 * row + h, 1), :])
                near[4 + h, 3 * i + c : 3 * i + c + 1, :] = jnp.where(count > 2, got, 0.0)
        at = slice(3 * i, 3 * i + 3)
        flag = lambda yes: jnp.full((3, 128), jnp.where(yes, F32(1.0), F32(0.0)))
        m16_ref[at, :] = flag((count > 3) & (three // fine == across))
        m17_ref[at, :] = flag((count > 3) & (three // fine != across))
    for i in range(blocks):
        at = slice(3 * i, 3 * i + 3)
        lhs = jnp.concatenate([near[n, at, :] for n in range(6)], axis=1).astype(BF16)
        acc_ref[at, :] = jnp.dot(lhs, weights_ref[i, 0:3].reshape(768, 128), preferred_element_type=F32)


def far_kernel(acc_ref, m16_ref, m17_ref, g16_ref, g17_ref, ang_ref, keep_ref, got_ref, weights_ref,
               out_ref, three, cart, wind):
    blocks, piece = weights_ref.shape[0], wind.shape[0]
    wide = lambda ref: jnp.concatenate([ref[...], ref[...]], axis=1) > 0.5
    three[...] = jnp.where(
        wide(m16_ref), g16_ref[...].astype(F32), jnp.where(wide(m17_ref), g17_ref[...].astype(F32), 0.0)
    )
    for i in range(blocks):
        at = slice(3 * i, 3 * i + 3)
        cart[at, :] = acc_ref[at, :] + jnp.dot(
            three[at, :].astype(BF16), weights_ref[i, 3], preferred_element_type=F32
        )
    x, y, z = (cart[pl.ds(c, blocks, stride=3), :] for c in range(3))
    first = lax.axis_index("mem") * piece
    sa, ca = sin_cos(ang_ref[pl.ds(first, blocks, stride=2), :])
    sp, cp = sin_cos(ang_ref[pl.ds(first + 1, blocks, stride=2), :])
    wind[pl.ds(0, blocks, stride=2), :] = -sa * x + ca * y
    wind[pl.ds(1, blocks, stride=2), :] = -sp * ca * x - sp * sa * y + cp * z
    total = keep_ref[...] + got_ref[...]
    for n in range(out_ref.shape[0]):
        out_ref[n, 0:piece, :] = wind[...]
        out_ref[n, piece:, :] = total


def out_kernel(members_ref, all_ref, out_ref, delta, buffer, sems):
    piece = delta.shape[0] // all_ref.shape[0]
    for h in range(2):
        for b in range(2):
            mean = (all_ref[4 * h + b, piece:, :] + all_ref[4 * h + b + 2, piece:, :]) / F32(80.0)
            first = 4 * h + 2 * b
            for n in range(2):
                at = slice((first + n) * piece, (first + n + 1) * piece)
                delta[at, :] = all_ref[first + n, 0:piece, :] - mean[n * piece : (n + 1) * piece, :]
    count = members_ref.shape[0]
    copies = [pltpu.make_async_copy(buffer.at[i], out_ref.at[i], sems.at[i]) for i in range(count)]
    for i in range(count):
        buffer[i] = members_ref[i] + delta[...]
        copies[i].start()
    for copy in copies:
        copy.wait()


def call(kernel, name, outs, specs, scratch=(), out_space=pltpu.VMEM, cost=1.0):
    shapes = tuple(out_space(shape, dtype) for shape, dtype in outs)
    out_specs = tuple(pl.BlockSpec(memory_space=out_space) for _ in outs)

    def run(*args):
        args = [placed(x, spec) for x, spec in zip(args, specs, strict=True)]
        return pl.pallas_call(
            kernel, out_shape=shapes, in_specs=specs, out_specs=out_specs, scratch_shapes=list(scratch), name=name,
            cost_estimate=pl.CostEstimate(flops=int(cost * 1e9), bytes_accessed=int(cost * 3.6e6), transcendentals=0),
            compiler_params=pltpu.CompilerParams(vmem_limit_bytes=8 * 2**20),
        )(*args)

    return run


def shards(members, increment, fine_angles, coarse_angles, remap_weights, sources, counts):
    mems, tiles = lax.axis_size("mem"), lax.axis_size("tile")
    weights = remap_weights[0]
    blocks = weights.shape[0]
    ids = sources[0].T
    flip = mems // 2
    far = tiles // 2

    def send(x, mem_flip, tile_shift):
        pairs = [
            (a * tiles + b, (a ^ mem_flip) * tiles + (b + tile_shift) % tiles)
            for a in range(mems)
            for b in range(tiles)
        ]
        return lax.ppermute(x, ("mem", "tile"), pairs)

    r17 = send(ids, flip, far + 1)
    r16 = send(ids, flip, far)

    inc_rows, ang_rows = flat(increment), flat(fine_angles)
    fine_rows = inc_rows.shape[0]
    cart, even = call(
        cart_kernel,
        "fine_cart",
        [((3, fine_rows, 128), F32), ((3, fine_rows // 2, 128), BF16)],
        [HBM, HBM],
        [pltpu.VMEM(inc_rows.shape, F32)] * 2 + [pltpu.SemaphoreType.DMA((4, 2))],
        cost=20,
    )(inc_rows, ang_rows)
    below = send(even, 0, 1)

    members_rows = flat(members)
    count, total_rows = members_rows.shape[:2]
    piece = total_rows // mems
    row = lambda n, dtype=F32: ((n, 128), dtype)
    members_rows, mine, other = call(
        sum_kernel,
        "member_sum",
        [(members_rows.shape, F32)] + [row(4 * piece)] * 2,
        [HBM, ANY],
        [pltpu.SemaphoreType.DMA((count, 2))],
        cost=20,
    )(members_rows, cart)
    got = send(other, flip, 0)

    rows = ((3 * blocks, 256), BF16)
    s17, s16 = call(
        pick_kernel,
        "pick_rows",
        [rows] * 2,
        [VMEM] * 3,
        [pltpu.SMEM((2,) + ids.shape, jnp.int32), pltpu.VMEM((2, 3 * blocks, 256), F32), pltpu.SemaphoreType.DMA((2,))],
        cost=20,
    )(r17, r16, cart)
    g17 = send(s17, flip, -(far + 1))
    g16 = send(s16, flip, -far)

    keep, other = call(pair_kernel, "pair_sum", [row(2 * piece)] * 2, [VMEM, VMEM, ANY])(mine, got, s17)
    got = send(other, 1, 0)

    near = call(
        near_kernel,
        "near_slots",
        [row(3 * blocks)] * 3,
        [SMEM, SMEM, VMEM, VMEM, VMEM],
        [pltpu.VMEM((6, 3 * blocks, 128), F32), pltpu.VMEM((3, fine_rows // 2, 128), F32)],
        cost=20,
    )(ids, counts, cart, below, weights)

    (payload,) = call(
        far_kernel,
        "far_slots",
        [((mems, 3 * piece, 128), F32)],
        [VMEM] * 9,
        [pltpu.VMEM((3 * blocks, 256), F32), pltpu.VMEM((3 * blocks, 128), F32), pltpu.VMEM((piece, 128), F32)],
    )(*near, g16, g17, flat(coarse_angles), keep, got, weights)
    payload = lax.all_to_all(payload, "mem", 0, 0, tiled=True)
    (out,) = call(
        out_kernel,
        "recentre",
        [(members_rows.shape, F32)],
        [VMEM, VMEM],
        [pltpu.VMEM((total_rows, 128), F32), pltpu.VMEM(members_rows.shape, F32), pltpu.SemaphoreType.DMA((count,))],
        pltpu.HBM,
    )(members_rows, payload)
    return unflat(out)


def solution(mesh):
    in_specs = (
        P("mem", None, "tile"),
        P(None, "tile"),
        P(None, "tile"),
        P(None, "tile"),
        P("tile", "mem", None, None, None),
        P("tile", "mem", None),
        P("tile", "mem"),
    )
    out_specs = P("mem", None, "tile")
    return jax.shard_map(shards, mesh=mesh, in_specs=in_specs, out_specs=out_specs, check_vma=False)
```

```python
import jax
import jax.numpy as jnp
from jax import lax
from jax.experimental import pallas as pl
from jax.experimental.pallas import tpu as pltpu
from jax.sharding import PartitionSpec as P

F32 = jnp.float32
BF16 = jnp.bfloat16
VMEM = pl.BlockSpec(memory_space=pltpu.VMEM)
SMEM = pl.BlockSpec(memory_space=pltpu.SMEM)
ANY = pl.BlockSpec(memory_space=pl.ANY)
HBM = pl.BlockSpec(memory_space=pltpu.HBM)


def placed(x, spec):
    if spec is VMEM:
        return pltpu.with_memory_space_constraint(x, pltpu.VMEM)
    return pltpu.with_memory_space_constraint(x, pltpu.HBM) if spec is HBM else x


def split(index, count, rows):
    return pl.ds(pl.multiple_of(index * rows, rows), rows)


def sin_cos(x):
    y = x * x
    s = F32(1.0 / 6227020800.0)
    for c in (-1.0 / 39916800.0, 1.0 / 362880.0, -1.0 / 5040.0, 1.0 / 120.0, -1.0 / 6.0):
        s = s * y + F32(c)
    c_ = F32(1.0 / 479001600.0)
    for c in (-1.0 / 3628800.0, 1.0 / 40320.0, -1.0 / 720.0, 1.0 / 24.0, -0.5):
        c_ = c_ * y + F32(c)
    return x + x * (y * s), F32(1.0) + y * c_


def flat(x):
    lead, columns = x.shape[:-2], x.shape[-1]
    chunks = columns // 128
    x = x.reshape(*lead, 2, chunks, 128)
    return jnp.swapaxes(x, -3, -2).reshape(*lead, 2 * chunks, 128)


def unflat(x):
    lead, rows = x.shape[:-2], x.shape[-2]
    x = x.reshape(*lead, rows // 2, 2, 128)
    return jnp.swapaxes(x, -3, -2).reshape(*lead, 2, rows * 64)


def pair_kernel(mine_ref, got_ref, after_ref, keep_ref, send_ref):
    del after_ref
    rows = keep_ref.shape[0]
    half = lax.rem(lax.axis_index("mem"), 2)
    for ref, part in ((keep_ref, half), (send_ref, 1 - half)):
        at = split(part, 2, rows)
        ref[...] = mine_ref[at, :] + got_ref[at, :]


def cart_kernel(inc_hbm, ang_hbm, cart_ref, even_ref, inc, ang, sems):
    parts = sems.shape[0]
    step = inc.shape[0] // parts
    loads = [
        [pltpu.make_async_copy(src.at[split(n, parts, step)], dst.at[split(n, parts, step)], sems.at[n, k])
         for k, (src, dst) in enumerate(((inc_hbm, inc), (ang_hbm, ang)))]
        for n in range(parts)
    ]
    for pair in loads:
        for load in pair:
            load.start()
    for n in range(parts):
        for load in loads[n]:
            load.wait()

        def body(k, carry, n=n):
            rows = 64
            at = pl.ds(pl.multiple_of(n * step + k * rows, rows), rows)
            s, c = sin_cos(ang[at, :].reshape(rows // 8, 8, 128))
            u = inc[at, :].reshape(rows // 8, 8, 128)
            su, cu = s * u, c * u
            t = pltpu.roll(su, 7, 1)
            cart_ref[0, at, :] = (-su - c * t).reshape(rows, 128)
            cart_ref[1, at, :] = (cu - s * t).reshape(rows, 128)
            cart_ref[2, at, :] = pltpu.roll(cu, 7, 1).reshape(rows, 128)
            return carry

        lax.fori_loop(0, step // 64, body, 0)
        half = step // 2
        for c in range(3):
            even_ref[c, n * half : (n + 1) * half, :] = cart_ref[c, pl.ds(n * step, half, stride=2), :].astype(BF16)


def first_kernel(inc_hbm, ang_hbm, members_hbm, cart_ref, even_ref, members_ref, inc, ang, odd, sems, member_sems):
    parts, count = sems.shape[0], members_hbm.shape[0]
    step = inc.shape[0] // parts
    loads = [
        [pltpu.make_async_copy(src.at[split(n, parts, step)], dst.at[split(n, parts, step)], sems.at[n, k])
         for k, (src, dst) in enumerate(((inc_hbm, inc), (ang_hbm, ang)))]
        for n in range(parts)
    ]
    member_loads = [
        pltpu.make_async_copy(members_hbm.at[n], members_ref.at[n], member_sems.at[n]) for n in range(count)
    ]
    for load in sum(loads, []) + member_loads:
        load.start()
    for n in range(parts):
        for load in loads[n]:
            load.wait()

        def body(k, carry, n=n):
            rows = 64
            at = pl.ds(pl.multiple_of(n * step + k * rows, rows), rows)
            s, c = sin_cos(ang[at, :].reshape(rows // 8, 8, 128))
            u = inc[at, :].reshape(rows // 8, 8, 128)
            su, cu = s * u, c * u
            t = pltpu.roll(su, 7, 1)
            odd[0, at, :] = (-su - c * t).reshape(rows, 128)
            odd[1, at, :] = (cu - s * t).reshape(rows, 128)
            odd[2, at, :] = pltpu.roll(cu, 7, 1).reshape(rows, 128)
            return carry

        lax.fori_loop(0, step // 64, body, 0)
        half = step // 2
        for c in range(3):
            kept = odd[c, pl.ds(n * step, half, stride=2), :]
            cart_ref[c, n * half : (n + 1) * half, :] = kept
            even_ref[c, n * half : (n + 1) * half, :] = kept.astype(BF16)
    for load in member_loads:
        load.wait()


def sum_kernel(members_ref, keep_ref, send_ref):
    rows = keep_ref.shape[0]
    half = lax.axis_index("mem") // 4
    keep_ref[...] = jnp.sum(members_ref[:, split(half, 2, rows), :], axis=0)
    send_ref[...] = jnp.sum(members_ref[:, split(1 - half, 2, rows), :], axis=0)


def pair_kernel(mine_ref, got_ref, after_ref, keep_ref, send_ref):
    del after_ref
    rows = keep_ref.shape[0]
    half = lax.rem(lax.axis_index("mem"), 2)
    for ref, part in ((keep_ref, half), (send_ref, 1 - half)):
        at = split(part, 2, rows)
        ref[...] = mine_ref[at, :] + got_ref[at, :]


def pick_kernel(r17_ref, r16_ref, cart_ref, s17_ref, s16_ref, ids, tmp, sems):
    fine = cart_ref.shape[1] // 2
    asked = ((r17_ref, 3, s17_ref), (r16_ref, 3, s16_ref))
    copies = [pltpu.make_async_copy(ref, ids.at[n], sems.at[n]) for n, (ref, _, _) in enumerate(asked)]
    for copy in copies:
        copy.start()
    for copy in copies:
        copy.wait()
    for n, (ref, slot, out) in enumerate(asked):
        for i in range(ref.shape[1]):
            row = 2 * (ids[n, slot, i] & (fine - 1))
            for c in range(3):
                for h in range(2):
                    tmp[n, 3 * i + c : 3 * i + c + 1, 128 * h : 128 * h + 128] = cart_ref[c, pl.ds(row + h, 1), :]
        out[...] = tmp[n].astype(BF16)


def near_kernel(ids_ref, counts_ref, cart_ref, below_ref, weights_ref, acc_ref, m17_ref, m16_ref, near, below):
    blocks = weights_ref.shape[0]
    fine = cart_ref.shape[1] // 2
    tiles = lax.axis_size("tile")
    tile = lax.axis_index("tile")
    across = lax.rem(tile + tiles // 2, tiles)
    first = pl.multiple_of(lax.axis_index("mem") * (blocks * 4), 8)
    below[...] = below_ref[...].astype(F32)
    for k in range(2):
        for c in range(3):
            for h in range(2):
                near[2 * k + h, pl.ds(c, blocks, stride=3), :] = (
                    cart_ref[c, pl.ds(first + 2 * k + h, blocks, stride=4), :]
                )
    for i in range(blocks):
        count, two, three = counts_ref[0, i], ids_ref[2, i], ids_ref[3, i]
        row, mine, straight = 2 * (two & (fine - 1)), two // fine == tile, three // fine == across
        for c in range(3):
            for h in range(2):
                got = jnp.where(mine, cart_ref[c, pl.ds(row + h, 1), :], below[c, pl.ds(row + h, 1), :])
                near[4 + h, 3 * i + c : 3 * i + c + 1, :] = jnp.where(count > 2, got, 0.0)
        at = slice(3 * i, 3 * i + 3)
        flag = lambda yes: jnp.full((3, 128), jnp.where(yes, F32(1.0), F32(0.0)))
        m17_ref[at, :] = flag((count > 3) & ~straight)
        m16_ref[at, :] = flag((count > 3) & straight)
    for i in range(blocks):
        at = slice(3 * i, 3 * i + 3)
        lhs = jnp.concatenate([near[n, at, :] for n in range(6)], axis=1).astype(BF16)
        acc_ref[at, :] = jnp.dot(lhs, weights_ref[i, 0:3].reshape(768, 128), preferred_element_type=F32)


def far_kernel(acc_ref, m17_ref, m16_ref, g17_ref, g16_ref, ang_ref, keep_ref, got_ref, weights_ref,
               out_ref, rows, cart, wind):
    blocks, piece = weights_ref.shape[0], wind.shape[0]
    wide = lambda ref: jnp.concatenate([ref[...], ref[...]], axis=1) > 0.5
    rows[...] = jnp.where(
        wide(m16_ref), g16_ref[...].astype(F32), jnp.where(wide(m17_ref), g17_ref[...].astype(F32), 0.0)
    )
    for i in range(blocks):
        at = slice(3 * i, 3 * i + 3)
        cart[at, :] = acc_ref[at, :] + jnp.dot(
            rows[at, :].astype(BF16), weights_ref[i, 3], preferred_element_type=F32
        )
    x, y, z = (cart[pl.ds(c, blocks, stride=3), :] for c in range(3))
    first = lax.axis_index("mem") * piece
    sa, ca = sin_cos(ang_ref[pl.ds(first, blocks, stride=2), :])
    sp, cp = sin_cos(ang_ref[pl.ds(first + 1, blocks, stride=2), :])
    wind[pl.ds(0, blocks, stride=2), :] = -sa * x + ca * y
    wind[pl.ds(1, blocks, stride=2), :] = -sp * ca * x - sp * sa * y + cp * z
    total = keep_ref[...] + got_ref[...]
    for n in range(out_ref.shape[0]):
        out_ref[n, 0:piece, :] = wind[...]
        out_ref[n, piece:, :] = total


def out_kernel(members_ref, all_ref, out_ref, delta, buffer, sems):
    piece = delta.shape[0] // all_ref.shape[0]
    for h in range(2):
        for b in range(2):
            mean = (all_ref[4 * h + b, piece:, :] + all_ref[4 * h + b + 2, piece:, :]) / F32(80.0)
            first = 4 * h + 2 * b
            for n in range(2):
                at = slice((first + n) * piece, (first + n + 1) * piece)
                delta[at, :] = all_ref[first + n, 0:piece, :] - mean[n * piece : (n + 1) * piece, :]
    count = members_ref.shape[0]
    copies = [pltpu.make_async_copy(buffer.at[i], out_ref.at[i], sems.at[i]) for i in range(count)]
    for i in range(count):
        buffer[i] = members_ref[i] + delta[...]
        copies[i].start()
    for copy in copies:
        copy.wait()


def call(kernel, name, outs, specs, scratch=(), out_space=pltpu.VMEM, cost=1.0):
    shapes = tuple(out_space(shape, dtype) for shape, dtype in outs)
    out_specs = tuple(pl.BlockSpec(memory_space=out_space) for _ in outs)

    def run(*args):
        args = [placed(x, spec) for x, spec in zip(args, specs, strict=True)]
        return pl.pallas_call(
            kernel, out_shape=shapes, in_specs=specs, out_specs=out_specs, scratch_shapes=list(scratch), name=name,
            cost_estimate=pl.CostEstimate(flops=int(cost * 1e9), bytes_accessed=int(cost * 3.6e6), transcendentals=0),
            compiler_params=pltpu.CompilerParams(vmem_limit_bytes=8 * 2**20),
        )(*args)

    return run


def shards(members, increment, fine_angles, coarse_angles, remap_weights, sources, counts):
    mems, tiles = lax.axis_size("mem"), lax.axis_size("tile")
    weights = remap_weights[0]
    blocks = weights.shape[0]
    ids = sources[0].T
    flip = mems // 2
    far = tiles // 2

    def send(x, mem_flip, tile_shift):
        pairs = [
            (a * tiles + b, (a ^ mem_flip) * tiles + (b + tile_shift) % tiles)
            for a in range(mems)
            for b in range(tiles)
        ]
        return lax.ppermute(x, ("mem", "tile"), pairs)

    def shifted(shift):
        pairs = []
        for a in range(mems):
            for b in range(tiles):
                c = (b + shift) % tiles
                near = a ^ flip if b // far != c // far else a
                pairs.append((a * tiles + b, near * tiles + c))
        return pairs

    axes = ("mem", "tile")
    p17, p16 = shifted(far + 1), shifted(far)
    r17, r16 = (lax.ppermute(ids, axes, p) for p in (p17, p16))

    inc_rows, ang_rows, members_rows = flat(increment), flat(fine_angles), flat(members)
    fine_rows = inc_rows.shape[0]
    count, total_rows = members_rows.shape[:2]
    piece = total_rows // mems
    row = lambda n, dtype=F32: ((n, 128), dtype)
    whole = (3, fine_rows // 2, 128)
    cart, even, members_rows = call(
        first_kernel,
        "fine_cart",
        [(whole, F32), (whole, BF16), (members_rows.shape, F32)],
        [HBM] * 3,
        [pltpu.VMEM(inc_rows.shape, F32)] * 2
        + [pltpu.VMEM((3, fine_rows, 128), F32), pltpu.SemaphoreType.DMA((4, 2)), pltpu.SemaphoreType.DMA((count,))],
        cost=20,
    )(inc_rows, ang_rows, members_rows)

    below = lax.ppermute(even, axes, shifted(1))

    mine, other = call(sum_kernel, "member_sum", [row(4 * piece)] * 2, [VMEM], cost=20)(members_rows)
    got = send(other, flip, 0)

    rows = ((3 * blocks, 256), BF16)
    s17, s16 = call(
        pick_kernel,
        "pick_rows",
        [rows] * 2,
        [VMEM] * 3,
        [pltpu.SMEM((2,) + ids.shape, jnp.int32), pltpu.VMEM((2, 3 * blocks, 256), F32), pltpu.SemaphoreType.DMA((2,))],
        cost=20,
    )(r17, r16, cart)
    g17, g16 = (lax.ppermute(x, axes, [(d, a) for a, d in p]) for x, p in ((s17, p17), (s16, p16)))

    keep, other = call(pair_kernel, "pair_sum", [row(2 * piece)] * 2, [VMEM, VMEM, ANY])(mine, got, s17)
    got = send(other, 1, 0)

    near = call(
        near_kernel,
        "near_slots",
        [row(3 * blocks)] * 3,
        [SMEM, SMEM, VMEM, VMEM, VMEM],
        [pltpu.VMEM((6, 3 * blocks, 128), F32), pltpu.VMEM(whole, F32)],
        cost=20,
    )(ids, counts, cart, below, weights)

    (payload,) = call(
        far_kernel,
        "far_slots",
        [((mems, 3 * piece, 128), F32)],
        [VMEM] * 9,
        [pltpu.VMEM((3 * blocks, 256), F32), pltpu.VMEM((3 * blocks, 128), F32), pltpu.VMEM((piece, 128), F32)],
    )(*near, g17, g16, flat(coarse_angles), keep, got, weights)
    payload = lax.all_to_all(payload, "mem", 0, 0, tiled=True)
    (out,) = call(
        out_kernel,
        "recentre",
        [(members_rows.shape, F32)],
        [VMEM, VMEM],
        [pltpu.VMEM((total_rows, 128), F32), pltpu.VMEM(members_rows.shape, F32), pltpu.SemaphoreType.DMA((count,))],
        pltpu.HBM,
    )(members_rows, payload)
    return unflat(out)


def solution(mesh):
    in_specs = (
        P("mem", None, "tile"),
        P(None, "tile"),
        P(None, "tile"),
        P(None, "tile"),
        P("tile", "mem", None, None, None),
        P("tile", "mem", None),
        P("tile", "mem"),
    )
    out_specs = P("mem", None, "tile")
    return jax.shard_map(shards, mesh=mesh, in_specs=in_specs, out_specs=out_specs, check_vma=False)
```

```python
import jax
import jax.numpy as jnp
from jax import lax
from jax.experimental import pallas as pl
from jax.experimental.pallas import tpu as pltpu
from jax.sharding import PartitionSpec as P

F32 = jnp.float32
BF16 = jnp.bfloat16
VMEM = pl.BlockSpec(memory_space=pltpu.VMEM)
SMEM = pl.BlockSpec(memory_space=pltpu.SMEM)
ANY = pl.BlockSpec(memory_space=pl.ANY)
HBM = pl.BlockSpec(memory_space=pltpu.HBM)


def placed(x, spec):
    if spec is VMEM:
        return pltpu.with_memory_space_constraint(x, pltpu.VMEM)
    return pltpu.with_memory_space_constraint(x, pltpu.HBM) if spec is HBM else x


def split(index, count, rows):
    return pl.ds(pl.multiple_of(index * rows, rows), rows)


def sin_cos(x):
    y = x * x
    s = F32(1.0 / 6227020800.0)
    for c in (-1.0 / 39916800.0, 1.0 / 362880.0, -1.0 / 5040.0, 1.0 / 120.0, -1.0 / 6.0):
        s = s * y + F32(c)
    c_ = F32(1.0 / 479001600.0)
    for c in (-1.0 / 3628800.0, 1.0 / 40320.0, -1.0 / 720.0, 1.0 / 24.0, -0.5):
        c_ = c_ * y + F32(c)
    return x + x * (y * s), F32(1.0) + y * c_


def flat(x):
    lead, columns = x.shape[:-2], x.shape[-1]
    chunks = columns // 128
    x = x.reshape(*lead, 2, chunks, 128)
    return jnp.swapaxes(x, -3, -2).reshape(*lead, 2 * chunks, 128)


def unflat(x):
    lead, rows = x.shape[:-2], x.shape[-2]
    x = x.reshape(*lead, rows // 2, 2, 128)
    return jnp.swapaxes(x, -3, -2).reshape(*lead, 2, rows * 64)


def pair_kernel(mine_ref, got_ref, after_ref, keep_ref, send_ref):
    del after_ref
    rows = keep_ref.shape[0]
    half = lax.rem(lax.axis_index("mem"), 2)
    for ref, part in ((keep_ref, half), (send_ref, 1 - half)):
        at = split(part, 2, rows)
        ref[...] = mine_ref[at, :] + got_ref[at, :]


def first_kernel(inc_hbm, ang_hbm, members_hbm, even_ref, members_ref, inc, ang, odd, sems, member_sems):
    parts, count = sems.shape[0], members_hbm.shape[0]
    step = inc.shape[0] // parts
    loads = [
        [pltpu.make_async_copy(src.at[split(n, parts, step)], dst.at[split(n, parts, step)], sems.at[n, k])
         for k, (src, dst) in enumerate(((inc_hbm, inc), (ang_hbm, ang)))]
        for n in range(parts)
    ]
    member_loads = [
        pltpu.make_async_copy(members_hbm.at[n], members_ref.at[n], member_sems.at[n]) for n in range(count)
    ]
    for load in sum(loads, []) + member_loads:
        load.start()
    for n in range(parts):
        for load in loads[n]:
            load.wait()

        def body(k, carry, n=n):
            rows = 64
            at = pl.ds(pl.multiple_of(n * step + k * rows, rows), rows)
            s, c = sin_cos(ang[at, :].reshape(rows // 8, 8, 128))
            u = inc[at, :].reshape(rows // 8, 8, 128)
            su, cu = s * u, c * u
            t = pltpu.roll(su, 7, 1)
            odd[0, at, :] = (-su - c * t).reshape(rows, 128)
            odd[1, at, :] = (cu - s * t).reshape(rows, 128)
            odd[2, at, :] = pltpu.roll(cu, 7, 1).reshape(rows, 128)
            return carry

        lax.fori_loop(0, step // 64, body, 0)
        half = step // 2
        for c in range(3):
            even_ref[c, n * half : (n + 1) * half, :] = odd[c, pl.ds(n * step, half, stride=2), :].astype(BF16)
    for load in member_loads:
        load.wait()


def sum_kernel(members_ref, keep_ref, send_ref):
    rows = keep_ref.shape[0]
    half = lax.axis_index("mem") // 4
    keep_ref[...] = jnp.sum(members_ref[:, split(half, 2, rows), :], axis=0)
    send_ref[...] = jnp.sum(members_ref[:, split(1 - half, 2, rows), :], axis=0)


def column(row):
    n = row.shape[1]
    wide = jnp.concatenate([row.astype(F32), jnp.zeros((1, 128 - n), F32)], axis=1)
    return jnp.transpose(jnp.broadcast_to(wide, (8, 128)))[0:n, 0:1]


def pick_kernel(r17_ref, r16_ref, even_ref, s17_ref, s16_ref):
    rows, blocks = even_ref.shape[1], r17_ref.shape[1]
    fine = rows // 2
    asked = jnp.concatenate([2 * (ref[3:4, :] & (fine - 1)) + h for ref in (r17_ref, r16_ref) for h in range(2)], axis=1)
    at = lax.broadcasted_iota(jnp.int32, (4 * blocks, rows), 1).astype(F32)
    chosen = jnp.where(at == column(asked), F32(1.0), F32(0.0)).astype(BF16)
    table = jnp.concatenate([even_ref[c] for c in range(3)], axis=1)
    got = jnp.dot(chosen, table, preferred_element_type=F32)
    for n, ref in enumerate((s17_ref, s16_ref)):
        for c in range(3):
            ref[2 * blocks * c : 2 * blocks * (c + 1), :] = (
                got[2 * blocks * n : 2 * blocks * (n + 1), 128 * c : 128 * (c + 1)].astype(ref.dtype)
            )


def near_kernel(ids_ref, counts_ref, even_ref, below_ref, weights_ref, acc_ref, from_ref, near, held):
    blocks, rows = weights_ref.shape[0], even_ref.shape[1]
    fine = rows // 2
    bits = fine.bit_length() - 1
    tiles = lax.axis_size("tile")
    tile = lax.axis_index("tile")
    across = lax.rem(tile + tiles // 2, tiles)
    first = split(lax.axis_index("mem"), 8, 4 * blocks)
    count, two, three = counts_ref[...], ids_ref[2:3, :], ids_ref[3:4, :]
    row = 2 * (two & (fine - 1)) + jnp.where((two >> bits) == tile, 0, rows)
    asked = [jnp.where(count > 2, row + h, -1) for h in range(2)]
    source = jnp.where(count > 3, jnp.where((three >> bits) == across, 1, 2), 0)
    numbers = column(jnp.concatenate(asked + [source], axis=1))
    from_ref[...] = jnp.broadcast_to(numbers[2 * blocks :], from_ref.shape)
    at = lax.broadcasted_iota(jnp.int32, (2 * blocks, 2 * rows), 1).astype(F32)
    chosen = jnp.where(at == numbers[: 2 * blocks], F32(1.0), F32(0.0)).astype(BF16)
    got = sum(
        jnp.dot(
            chosen[:, rows * n : rows * (n + 1)],
            jnp.concatenate([ref[c] for c in range(3)], axis=1),
            preferred_element_type=F32,
        )
        for n, ref in enumerate((even_ref, below_ref))
    )
    for c in range(3):
        held[c] = even_ref[c, first, :].astype(F32)
        for h in range(2):
            for k in range(2):
                near[2 * k + h, pl.ds(c, blocks, stride=3), :] = held[c, pl.ds(2 * k + h, blocks, stride=4), :]
            near[4 + h, pl.ds(c, blocks, stride=3), :] = got[blocks * h : blocks * (h + 1), 128 * c : 128 * (c + 1)]
    for i in range(blocks):
        at = slice(3 * i, 3 * i + 3)
        lhs = jnp.concatenate([near[n, at, :] for n in range(6)], axis=1).astype(BF16)
        acc_ref[at, :] = jnp.dot(lhs, weights_ref[i, 0:3].reshape(768, 128), preferred_element_type=F32)


def far_kernel(acc_ref, from_ref, g17_ref, g16_ref, ang_ref, keep_ref, got_ref, weights_ref,
               out_ref, rows, cart, wind):
    blocks, piece = weights_ref.shape[0], wind.shape[0]
    from17 = from_ref[...] > 1.5
    from16 = (from_ref[...] > 0.5) & ~from17
    for c in range(3):
        for h in range(2):
            at = slice(blocks * (2 * c + h), blocks * (2 * c + h + 1))
            rows[h, pl.ds(c, blocks, stride=3), :] = jnp.where(
                from16, g16_ref[at, :].astype(F32), jnp.where(from17, g17_ref[at, :].astype(F32), 0.0)
            )
    for i in range(blocks):
        at = slice(3 * i, 3 * i + 3)
        cart[at, :] = acc_ref[at, :] + jnp.dot(
            jnp.concatenate([rows[0, at, :], rows[1, at, :]], axis=1).astype(BF16),
            weights_ref[i, 3],
            preferred_element_type=F32,
        )
    x, y, z = (cart[pl.ds(c, blocks, stride=3), :] for c in range(3))
    first = lax.axis_index("mem") * piece
    sa, ca = sin_cos(ang_ref[pl.ds(first, blocks, stride=2), :])
    sp, cp = sin_cos(ang_ref[pl.ds(first + 1, blocks, stride=2), :])
    wind[pl.ds(0, blocks, stride=2), :] = -sa * x + ca * y
    wind[pl.ds(1, blocks, stride=2), :] = -sp * ca * x - sp * sa * y + cp * z
    total = keep_ref[...] + got_ref[...]
    for n in range(out_ref.shape[0]):
        out_ref[n, 0:piece, :] = wind[...]
        out_ref[n, piece:, :] = total


def out_kernel(members_ref, all_ref, out_ref, delta, buffer, sems):
    piece = delta.shape[0] // all_ref.shape[0]
    for h in range(2):
        for b in range(2):
            mean = (all_ref[4 * h + b, piece:, :] + all_ref[4 * h + b + 2, piece:, :]) / F32(80.0)
            first = 4 * h + 2 * b
            for n in range(2):
                at = slice((first + n) * piece, (first + n + 1) * piece)
                delta[at, :] = all_ref[first + n, 0:piece, :] - mean[n * piece : (n + 1) * piece, :]
    count = members_ref.shape[0]
    copies = [pltpu.make_async_copy(buffer.at[i], out_ref.at[i], sems.at[i]) for i in range(count)]
    for i in range(count):
        buffer[i] = members_ref[i] + delta[...]
        copies[i].start()
    for copy in copies:
        copy.wait()


def call(kernel, name, outs, specs, scratch=(), out_space=pltpu.VMEM, cost=1.0):
    shapes = tuple(out_space(shape, dtype) for shape, dtype in outs)
    out_specs = tuple(pl.BlockSpec(memory_space=out_space) for _ in outs)

    def run(*args):
        args = [placed(x, spec) for x, spec in zip(args, specs, strict=True)]
        return pl.pallas_call(
            kernel, out_shape=shapes, in_specs=specs, out_specs=out_specs, scratch_shapes=list(scratch), name=name,
            cost_estimate=pl.CostEstimate(flops=int(cost * 1e9), bytes_accessed=int(cost * 3.6e6), transcendentals=0),
            compiler_params=pltpu.CompilerParams(vmem_limit_bytes=8 * 2**20),
        )(*args)

    return run


def shards(members, increment, fine_angles, coarse_angles, remap_weights, sources, counts):
    mems, tiles = lax.axis_size("mem"), lax.axis_size("tile")
    weights = remap_weights[0]
    blocks = weights.shape[0]
    ids = sources[0].T
    flip = mems // 2
    far = tiles // 2

    def send(x, mem_flip, tile_shift):
        pairs = [
            (a * tiles + b, (a ^ mem_flip) * tiles + (b + tile_shift) % tiles)
            for a in range(mems)
            for b in range(tiles)
        ]
        return lax.ppermute(x, ("mem", "tile"), pairs)

    def shifted(shift):
        pairs = []
        for a in range(mems):
            for b in range(tiles):
                c = (b + shift) % tiles
                near = a ^ flip if b // far != c // far else a
                pairs.append((a * tiles + b, near * tiles + c))
        return pairs

    axes = ("mem", "tile")
    p17, p16 = shifted(far + 1), shifted(far)
    r17, r16 = (lax.ppermute(ids, axes, p) for p in (p17, p16))

    inc_rows, ang_rows, members_rows = flat(increment), flat(fine_angles), flat(members)
    fine_rows = inc_rows.shape[0]
    count, total_rows = members_rows.shape[:2]
    piece = total_rows // mems
    row = lambda n, dtype=F32: ((n, 128), dtype)
    whole = (3, fine_rows // 2, 128)
    even, members_rows = call(
        first_kernel,
        "fine_cart",
        [(whole, BF16), (members_rows.shape, F32)],
        [HBM] * 3,
        [pltpu.VMEM(inc_rows.shape, F32)] * 2
        + [pltpu.VMEM((3, fine_rows, 128), F32), pltpu.SemaphoreType.DMA((4, 2)), pltpu.SemaphoreType.DMA((count,))],
        cost=20,
    )(inc_rows, ang_rows, members_rows)

    below = lax.ppermute(even, axes, shifted(1))

    mine, other = call(sum_kernel, "member_sum", [row(4 * piece)] * 2, [VMEM], cost=20)(members_rows)
    got = send(other, flip, 0)

    rows = (6 * blocks, 128)
    s17, s16 = call(pick_kernel, "pick_rows", [(rows, BF16), (rows, BF16)], [VMEM] * 3, cost=2)(r17, r16, even)
    g17, g16 = (lax.ppermute(x, axes, [(d, a) for a, d in p]) for x, p in ((s17, p17), (s16, p16)))

    keep, other = call(pair_kernel, "pair_sum", [row(2 * piece)] * 2, [VMEM, VMEM, ANY])(mine, got, s16)
    got = send(other, 1, 0)

    near = call(
        near_kernel,
        "near_slots",
        [row(3 * blocks), row(blocks)],
        [VMEM] * 5,
        [pltpu.VMEM((6, 3 * blocks, 128), F32), pltpu.VMEM((3, 4 * blocks, 128), F32)],
        cost=20,
    )(ids, counts, even, below, weights)

    (payload,) = call(
        far_kernel,
        "far_slots",
        [((mems, 3 * piece, 128), F32)],
        [VMEM] * 8,
        [pltpu.VMEM((2, 3 * blocks, 128), F32), pltpu.VMEM((3 * blocks, 128), F32), pltpu.VMEM((piece, 128), F32)],
    )(*near, g17, g16, flat(coarse_angles), keep, got, weights)
    payload = lax.all_to_all(payload, "mem", 0, 0, tiled=True)
    (out,) = call(
        out_kernel,
        "recentre",
        [(members_rows.shape, F32)],
        [VMEM, VMEM],
        [pltpu.VMEM((total_rows, 128), F32), pltpu.VMEM(members_rows.shape, F32), pltpu.SemaphoreType.DMA((count,))],
        pltpu.HBM,
    )(members_rows, payload)
    return unflat(out)


def solution(mesh):
    in_specs = (
        P("mem", None, "tile"),
        P(None, "tile"),
        P(None, "tile"),
        P(None, "tile"),
        P("tile", "mem", None, None, None),
        P("tile", "mem", None),
        P("tile", "mem"),
    )
    out_specs = P("mem", None, "tile")
    return jax.shard_map(shards, mesh=mesh, in_specs=in_specs, out_specs=out_specs, check_vma=False)
```

```python
import jax
import jax.numpy as jnp
from jax import lax
from jax.experimental import pallas as pl
from jax.experimental.pallas import tpu as pltpu
from jax.sharding import PartitionSpec as P

F32 = jnp.float32
BF16 = jnp.bfloat16
VMEM = pl.BlockSpec(memory_space=pltpu.VMEM)
SMEM = pl.BlockSpec(memory_space=pltpu.SMEM)
ANY = pl.BlockSpec(memory_space=pl.ANY)
HBM = pl.BlockSpec(memory_space=pltpu.HBM)


def placed(x, spec):
    if spec is VMEM:
        return pltpu.with_memory_space_constraint(x, pltpu.VMEM)
    return pltpu.with_memory_space_constraint(x, pltpu.HBM) if spec is HBM else x


def split(index, count, rows):
    return pl.ds(pl.multiple_of(index * rows, rows), rows)


def sin_cos(x):
    y = x * x
    s = F32(1.0 / 6227020800.0)
    for c in (-1.0 / 39916800.0, 1.0 / 362880.0, -1.0 / 5040.0, 1.0 / 120.0, -1.0 / 6.0):
        s = s * y + F32(c)
    c_ = F32(1.0 / 479001600.0)
    for c in (-1.0 / 3628800.0, 1.0 / 40320.0, -1.0 / 720.0, 1.0 / 24.0, -0.5):
        c_ = c_ * y + F32(c)
    return x + x * (y * s), F32(1.0) + y * c_


def flat(x):
    lead, columns = x.shape[:-2], x.shape[-1]
    chunks = columns // 128
    x = x.reshape(*lead, 2, chunks, 128)
    return jnp.swapaxes(x, -3, -2).reshape(*lead, 2 * chunks, 128)


def unflat(x):
    lead, rows = x.shape[:-2], x.shape[-2]
    x = x.reshape(*lead, rows // 2, 2, 128)
    return jnp.swapaxes(x, -3, -2).reshape(*lead, 2, rows * 64)


def pair_kernel(mine_ref, got_ref, after_ref, keep_ref, send_ref):
    del after_ref
    rows = keep_ref.shape[0]
    half = lax.rem(lax.axis_index("mem"), 2)
    for ref, part in ((keep_ref, half), (send_ref, 1 - half)):
        at = split(part, 2, rows)
        ref[...] = mine_ref[at, :] + got_ref[at, :]


def first_kernel(inc_hbm, ang_hbm, members_hbm, even_ref, members_ref, inc, ang, odd, sems, member_sems):
    parts, groups = sems.shape[0], member_sems.shape[0]
    each = members_hbm.shape[0] // groups
    step = inc.shape[0] // parts
    loads = [
        [pltpu.make_async_copy(src.at[split(n, parts, step)], dst.at[split(n, parts, step)], sems.at[n, k])
         for k, (src, dst) in enumerate(((inc_hbm, inc), (ang_hbm, ang)))]
        for n in range(parts)
    ]
    member_loads = [
        pltpu.make_async_copy(members_hbm.at[pl.ds(each * n, each)], members_ref.at[pl.ds(each * n, each)], member_sems.at[n])
        for n in range(groups)
    ]
    for load in sum(loads, []) + member_loads:
        load.start()
    for n in range(parts):
        for load in loads[n]:
            load.wait()

        def body(k, carry, n=n):
            rows = 64
            at = pl.ds(pl.multiple_of(n * step + k * rows, rows), rows)
            s, c = sin_cos(ang[at, :].reshape(rows // 8, 8, 128))
            u = inc[at, :].reshape(rows // 8, 8, 128)
            su, cu = s * u, c * u
            t = pltpu.roll(su, 7, 1)
            odd[0, at, :] = (-su - c * t).reshape(rows, 128)
            odd[1, at, :] = (cu - s * t).reshape(rows, 128)
            odd[2, at, :] = pltpu.roll(cu, 7, 1).reshape(rows, 128)
            return carry

        lax.fori_loop(0, step // 64, body, 0)
        half = step // 2
        for c in range(3):
            even_ref[c, n * half : (n + 1) * half, :] = odd[c, pl.ds(n * step, half, stride=2), :].astype(BF16)
    for load in member_loads:
        load.wait()


def sum_kernel(members_ref, keep_ref, send_ref):
    rows = keep_ref.shape[0]
    half = lax.axis_index("mem") // 4
    keep_ref[...] = jnp.sum(members_ref[:, split(half, 2, rows), :], axis=0)
    send_ref[...] = jnp.sum(members_ref[:, split(1 - half, 2, rows), :], axis=0)


def column(row):
    n = row.shape[1]
    wide = jnp.concatenate([row.astype(F32), jnp.zeros((1, 128 - n), F32)], axis=1)
    return jnp.transpose(jnp.broadcast_to(wide, (8, 128)))[0:n, 0:1]


def pick_kernel(r17_ref, r16_ref, even_ref, s17_ref, s16_ref):
    rows, blocks = even_ref.shape[1], r17_ref.shape[1]
    fine = rows // 2
    asked = jnp.concatenate([2 * (ref[3:4, :] & (fine - 1)) + h for ref in (r17_ref, r16_ref) for h in range(2)], axis=1)
    at = lax.broadcasted_iota(jnp.int32, (4 * blocks, rows), 1).astype(F32)
    chosen = jnp.where(at == column(asked), F32(1.0), F32(0.0)).astype(BF16)
    table = jnp.concatenate([even_ref[c] for c in range(3)], axis=1)
    got = jnp.dot(chosen, table, preferred_element_type=F32)
    for n, ref in enumerate((s17_ref, s16_ref)):
        for c in range(3):
            ref[2 * blocks * c : 2 * blocks * (c + 1), :] = (
                got[2 * blocks * n : 2 * blocks * (n + 1), 128 * c : 128 * (c + 1)].astype(ref.dtype)
            )


def near_kernel(ids_ref, counts_ref, even_ref, below_ref, weights_ref, acc_ref, from_ref, near, held):
    blocks, rows = weights_ref.shape[0], even_ref.shape[1]
    fine = rows // 2
    bits = fine.bit_length() - 1
    tiles = lax.axis_size("tile")
    tile = lax.axis_index("tile")
    across = lax.rem(tile + tiles // 2, tiles)
    first = split(lax.axis_index("mem"), 8, 4 * blocks)
    count, two, three = counts_ref[...], ids_ref[2:3, :], ids_ref[3:4, :]
    row = 2 * (two & (fine - 1)) + jnp.where((two >> bits) == tile, 0, rows)
    asked = [jnp.where(count > 2, row + h, -1) for h in range(2)]
    source = jnp.where(count > 3, jnp.where((three >> bits) == across, 1, 2), 0)
    numbers = column(jnp.concatenate(asked + [source], axis=1))
    from_ref[...] = jnp.broadcast_to(numbers[2 * blocks :], from_ref.shape)
    at = lax.broadcasted_iota(jnp.int32, (2 * blocks, 2 * rows), 1).astype(F32)
    chosen = jnp.where(at == numbers[: 2 * blocks], F32(1.0), F32(0.0)).astype(BF16)
    got = sum(
        jnp.dot(
            chosen[:, rows * n : rows * (n + 1)],
            jnp.concatenate([ref[c] for c in range(3)], axis=1),
            preferred_element_type=F32,
        )
        for n, ref in enumerate((even_ref, below_ref))
    )
    for c in range(3):
        held[c] = even_ref[c, first, :].astype(F32)
        for h in range(2):
            for k in range(2):
                near[2 * k + h, pl.ds(c, blocks, stride=3), :] = held[c, pl.ds(2 * k + h, blocks, stride=4), :]
            near[4 + h, pl.ds(c, blocks, stride=3), :] = got[blocks * h : blocks * (h + 1), 128 * c : 128 * (c + 1)]
    for i in range(blocks):
        at = slice(3 * i, 3 * i + 3)
        lhs = jnp.concatenate([near[n, at, :] for n in range(6)], axis=1).astype(BF16)
        acc_ref[at, :] = jnp.dot(lhs, weights_ref[i, 0:3].reshape(768, 128), preferred_element_type=F32)


def far_kernel(acc_ref, from_ref, g17_ref, g16_ref, ang_ref, keep_ref, got_ref, weights_ref,
               out_ref, rows, cart, wind):
    blocks, piece = weights_ref.shape[0], wind.shape[0]
    from17 = from_ref[...] > 1.5
    from16 = (from_ref[...] > 0.5) & ~from17
    for c in range(3):
        for h in range(2):
            at = slice(blocks * (2 * c + h), blocks * (2 * c + h + 1))
            rows[h, pl.ds(c, blocks, stride=3), :] = jnp.where(
                from16, g16_ref[at, :].astype(F32), jnp.where(from17, g17_ref[at, :].astype(F32), 0.0)
            )
    for i in range(blocks):
        at = slice(3 * i, 3 * i + 3)
        cart[at, :] = acc_ref[at, :] + jnp.dot(
            jnp.concatenate([rows[0, at, :], rows[1, at, :]], axis=1).astype(BF16),
            weights_ref[i, 3],
            preferred_element_type=F32,
        )
    x, y, z = (cart[pl.ds(c, blocks, stride=3), :] for c in range(3))
    first = lax.axis_index("mem") * piece
    sa, ca = sin_cos(ang_ref[pl.ds(first, blocks, stride=2), :])
    sp, cp = sin_cos(ang_ref[pl.ds(first + 1, blocks, stride=2), :])
    wind[pl.ds(0, blocks, stride=2), :] = -sa * x + ca * y
    wind[pl.ds(1, blocks, stride=2), :] = -sp * ca * x - sp * sa * y + cp * z
    total = keep_ref[...] + got_ref[...]
    for n in range(out_ref.shape[0]):
        out_ref[n, 0:piece, :] = wind[...]
        out_ref[n, piece:, :] = total


def out_kernel(members_ref, all_ref, out_ref, delta, buffer, sems):
    piece = delta.shape[0] // all_ref.shape[0]
    for h in range(2):
        for b in range(2):
            mean = (all_ref[4 * h + b, piece:, :] + all_ref[4 * h + b + 2, piece:, :]) / F32(80.0)
            first = 4 * h + 2 * b
            for n in range(2):
                at = slice((first + n) * piece, (first + n + 1) * piece)
                delta[at, :] = all_ref[first + n, 0:piece, :] - mean[n * piece : (n + 1) * piece, :]
    groups = sems.shape[0]
    each = members_ref.shape[0] // groups
    copies = [
        pltpu.make_async_copy(buffer.at[pl.ds(each * n, each)], out_ref.at[pl.ds(each * n, each)], sems.at[n])
        for n in range(groups)
    ]
    for n in range(groups):
        for i in range(each * n, each * (n + 1)):
            buffer[i] = members_ref[i] + delta[...]
        copies[n].start()
    for copy in copies:
        copy.wait()


def call(kernel, name, outs, specs, scratch=(), out_space=pltpu.VMEM, cost=1.0):
    shapes = tuple(out_space(shape, dtype) for shape, dtype in outs)
    out_specs = tuple(pl.BlockSpec(memory_space=out_space) for _ in outs)

    def run(*args):
        args = [placed(x, spec) for x, spec in zip(args, specs, strict=True)]
        return pl.pallas_call(
            kernel, out_shape=shapes, in_specs=specs, out_specs=out_specs, scratch_shapes=list(scratch), name=name,
            cost_estimate=pl.CostEstimate(flops=int(cost * 1e9), bytes_accessed=int(cost * 3.6e6), transcendentals=0),
            compiler_params=pltpu.CompilerParams(vmem_limit_bytes=8 * 2**20),
        )(*args)

    return run


def shards(members, increment, fine_angles, coarse_angles, remap_weights, sources, counts):
    mems, tiles = lax.axis_size("mem"), lax.axis_size("tile")
    weights = remap_weights[0]
    blocks = weights.shape[0]
    ids = sources[0].T
    flip = mems // 2
    far = tiles // 2

    def send(x, mem_flip, tile_shift):
        pairs = [
            (a * tiles + b, (a ^ mem_flip) * tiles + (b + tile_shift) % tiles)
            for a in range(mems)
            for b in range(tiles)
        ]
        return lax.ppermute(x, ("mem", "tile"), pairs)

    def shifted(shift):
        pairs = []
        for a in range(mems):
            for b in range(tiles):
                c = (b + shift) % tiles
                near = a ^ flip if b // far != c // far else a
                pairs.append((a * tiles + b, near * tiles + c))
        return pairs

    axes = ("mem", "tile")
    p17, p16 = shifted(far + 1), shifted(far)
    r17, r16 = (lax.ppermute(ids, axes, p) for p in (p17, p16))

    inc_rows, ang_rows, members_rows = flat(increment), flat(fine_angles), flat(members)
    fine_rows = inc_rows.shape[0]
    count, total_rows = members_rows.shape[:2]
    piece = total_rows // mems
    row = lambda n, dtype=F32: ((n, 128), dtype)
    whole = (3, fine_rows // 2, 128)
    even, members_rows = call(
        first_kernel,
        "fine_cart",
        [(whole, BF16), (members_rows.shape, F32)],
        [HBM] * 3,
        [pltpu.VMEM(inc_rows.shape, F32)] * 2
        + [pltpu.VMEM((3, fine_rows, 128), F32), pltpu.SemaphoreType.DMA((4, 2)), pltpu.SemaphoreType.DMA((1,))],
        cost=20,
    )(inc_rows, ang_rows, members_rows)

    below = lax.ppermute(even, axes, shifted(1))

    mine, other = call(sum_kernel, "member_sum", [row(4 * piece)] * 2, [VMEM], cost=20)(members_rows)
    got = send(other, flip, 0)

    rows = (6 * blocks, 128)
    s17, s16 = call(pick_kernel, "pick_rows", [(rows, BF16), (rows, BF16)], [VMEM] * 3, cost=2)(r17, r16, even)
    g17, g16 = (lax.ppermute(x, axes, [(d, a) for a, d in p]) for x, p in ((s17, p17), (s16, p16)))

    keep, other = call(pair_kernel, "pair_sum", [row(2 * piece)] * 2, [VMEM, VMEM, ANY])(mine, got, s16)
    got = send(other, 1, 0)

    near = call(
        near_kernel,
        "near_slots",
        [row(3 * blocks), row(blocks)],
        [VMEM] * 5,
        [pltpu.VMEM((6, 3 * blocks, 128), F32), pltpu.VMEM((3, 4 * blocks, 128), F32)],
        cost=20,
    )(ids, counts, even, below, weights)

    (payload,) = call(
        far_kernel,
        "far_slots",
        [((mems, 3 * piece, 128), F32)],
        [VMEM] * 8,
        [pltpu.VMEM((2, 3 * blocks, 128), F32), pltpu.VMEM((3 * blocks, 128), F32), pltpu.VMEM((piece, 128), F32)],
    )(*near, g17, g16, flat(coarse_angles), keep, got, weights)
    payload = lax.all_to_all(payload, "mem", 0, 0, tiled=True)
    (out,) = call(
        out_kernel,
        "recentre",
        [(members_rows.shape, F32)],
        [VMEM, VMEM],
        [pltpu.VMEM((total_rows, 128), F32), pltpu.VMEM(members_rows.shape, F32), pltpu.SemaphoreType.DMA((1,))],
        pltpu.HBM,
    )(members_rows, payload)
    return unflat(out)


def solution(mesh):
    in_specs = (
        P("mem", None, "tile"),
        P(None, "tile"),
        P(None, "tile"),
        P(None, "tile"),
        P("tile", "mem", None, None, None),
        P("tile", "mem", None),
        P("tile", "mem"),
    )
    out_specs = P("mem", None, "tile")
    return jax.shard_map(shards, mesh=mesh, in_specs=in_specs, out_specs=out_specs, check_vma=False)
```

```python
import jax
import jax.numpy as jnp
from jax import lax
from jax.experimental import pallas as pl
from jax.experimental.pallas import tpu as pltpu
from jax.sharding import PartitionSpec as P

F32 = jnp.float32
BF16 = jnp.bfloat16
VMEM = pl.BlockSpec(memory_space=pltpu.VMEM)
SMEM = pl.BlockSpec(memory_space=pltpu.SMEM)
ANY = pl.BlockSpec(memory_space=pl.ANY)
HBM = pl.BlockSpec(memory_space=pltpu.HBM)


def placed(x, spec):
    if spec is VMEM:
        return pltpu.with_memory_space_constraint(x, pltpu.VMEM)
    return pltpu.with_memory_space_constraint(x, pltpu.HBM) if spec is HBM else x


def split(index, count, rows):
    return pl.ds(pl.multiple_of(index * rows, rows), rows)


def sin_cos(x):
    y = x * x
    s = F32(1.0 / 6227020800.0)
    for c in (-1.0 / 39916800.0, 1.0 / 362880.0, -1.0 / 5040.0, 1.0 / 120.0, -1.0 / 6.0):
        s = s * y + F32(c)
    c_ = F32(1.0 / 479001600.0)
    for c in (-1.0 / 3628800.0, 1.0 / 40320.0, -1.0 / 720.0, 1.0 / 24.0, -0.5):
        c_ = c_ * y + F32(c)
    return x + x * (y * s), F32(1.0) + y * c_


def flat(x):
    lead, columns = x.shape[:-2], x.shape[-1]
    chunks = columns // 128
    x = x.reshape(*lead, 2, chunks, 128)
    return jnp.swapaxes(x, -3, -2).reshape(*lead, 2 * chunks, 128)


def unflat(x):
    lead, rows = x.shape[:-2], x.shape[-2]
    x = x.reshape(*lead, rows // 2, 2, 128)
    return jnp.swapaxes(x, -3, -2).reshape(*lead, 2, rows * 64)


def pair_kernel(mine_ref, got_ref, after_ref, keep_ref, send_ref):
    del after_ref
    rows = keep_ref.shape[0]
    half = lax.rem(lax.axis_index("mem"), 2)
    for ref, part in ((keep_ref, half), (send_ref, 1 - half)):
        at = split(part, 2, rows)
        ref[...] = mine_ref[at, :] + got_ref[at, :]


def first_kernel(inc_hbm, ang_hbm, members_hbm, even_ref, members_ref, keep_ref, send_ref,
                 inc, ang, odd, sems, member_sems):
    parts, groups = sems.shape[0], member_sems.shape[0]
    each = members_hbm.shape[0] // groups
    step = inc.shape[0] // parts
    loads = [
        [pltpu.make_async_copy(src.at[split(n, parts, step)], dst.at[split(n, parts, step)], sems.at[n, k])
         for k, (src, dst) in enumerate(((inc_hbm, inc), (ang_hbm, ang)))]
        for n in range(parts)
    ]
    member_loads = [
        pltpu.make_async_copy(members_hbm.at[pl.ds(each * n, each)], members_ref.at[pl.ds(each * n, each)], member_sems.at[n])
        for n in range(groups)
    ]
    for load in sum(loads, []) + member_loads:
        load.start()
    for n in range(parts):
        for load in loads[n]:
            load.wait()

        def body(k, carry, n=n):
            rows = 64
            at = pl.ds(pl.multiple_of(n * step + k * rows, rows), rows)
            s, c = sin_cos(ang[at, :].reshape(rows // 8, 8, 128))
            u = inc[at, :].reshape(rows // 8, 8, 128)
            su, cu = s * u, c * u
            t = pltpu.roll(su, 7, 1)
            odd[0, at, :] = (-su - c * t).reshape(rows, 128)
            odd[1, at, :] = (cu - s * t).reshape(rows, 128)
            odd[2, at, :] = pltpu.roll(cu, 7, 1).reshape(rows, 128)
            return carry

        lax.fori_loop(0, step // 64, body, 0)
        half = step // 2
        for c in range(3):
            even_ref[c, n * half : (n + 1) * half, :] = odd[c, pl.ds(n * step, half, stride=2), :].astype(BF16)
    for load in member_loads:
        load.wait()
    held = keep_ref.shape[0]
    group = lax.axis_index("mem") // 4
    send_ref[...] = jnp.sum(members_ref[:, split(1 - group, 2, held), :], axis=0)
    keep_ref[...] = jnp.sum(members_ref[:, split(group, 2, held), :], axis=0)


def column(row):
    n = row.shape[1]
    wide = jnp.concatenate([row.astype(F32), jnp.zeros((1, 128 - n), F32)], axis=1)
    return jnp.transpose(jnp.broadcast_to(wide, (8, 128)))[0:n, 0:1]


def pick_kernel(r17_ref, r16_ref, even_ref, s17_ref, s16_ref):
    rows, blocks = even_ref.shape[1], r17_ref.shape[1]
    fine = rows // 2
    asked = jnp.concatenate([2 * (ref[3:4, :] & (fine - 1)) + h for ref in (r17_ref, r16_ref) for h in range(2)], axis=1)
    at = lax.broadcasted_iota(jnp.int32, (4 * blocks, rows), 1).astype(F32)
    chosen = jnp.where(at == column(asked), F32(1.0), F32(0.0)).astype(BF16)
    table = jnp.concatenate([even_ref[c] for c in range(3)], axis=1)
    got = jnp.dot(chosen, table, preferred_element_type=F32)
    for n, ref in enumerate((s17_ref, s16_ref)):
        for c in range(3):
            ref[2 * blocks * c : 2 * blocks * (c + 1), :] = (
                got[2 * blocks * n : 2 * blocks * (n + 1), 128 * c : 128 * (c + 1)].astype(ref.dtype)
            )


def near_kernel(ids_ref, counts_ref, even_ref, below_ref, weights_ref, acc_ref, from_ref, near, held):
    blocks, rows = weights_ref.shape[0], even_ref.shape[1]
    fine = rows // 2
    bits = fine.bit_length() - 1
    tiles = lax.axis_size("tile")
    tile = lax.axis_index("tile")
    across = lax.rem(tile + tiles // 2, tiles)
    first = split(lax.axis_index("mem"), 8, 4 * blocks)
    count, two, three = counts_ref[...], ids_ref[2:3, :], ids_ref[3:4, :]
    row = 2 * (two & (fine - 1)) + jnp.where((two >> bits) == tile, 0, rows)
    asked = [jnp.where(count > 2, row + h, -1) for h in range(2)]
    source = jnp.where(count > 3, jnp.where((three >> bits) == across, 1, 2), 0)
    numbers = column(jnp.concatenate(asked + [source], axis=1))
    from_ref[...] = jnp.broadcast_to(numbers[2 * blocks :], from_ref.shape)
    at = lax.broadcasted_iota(jnp.int32, (2 * blocks, 2 * rows), 1).astype(F32)
    chosen = jnp.where(at == numbers[: 2 * blocks], F32(1.0), F32(0.0)).astype(BF16)
    got = sum(
        jnp.dot(
            chosen[:, rows * n : rows * (n + 1)],
            jnp.concatenate([ref[c] for c in range(3)], axis=1),
            preferred_element_type=F32,
        )
        for n, ref in enumerate((even_ref, below_ref))
    )
    for c in range(3):
        held[c] = even_ref[c, first, :].astype(F32)
        for h in range(2):
            for k in range(2):
                near[2 * k + h, pl.ds(c, blocks, stride=3), :] = held[c, pl.ds(2 * k + h, blocks, stride=4), :]
            near[4 + h, pl.ds(c, blocks, stride=3), :] = got[blocks * h : blocks * (h + 1), 128 * c : 128 * (c + 1)]
    for i in range(blocks):
        at = slice(3 * i, 3 * i + 3)
        lhs = jnp.concatenate([near[n, at, :] for n in range(6)], axis=1).astype(BF16)
        acc_ref[at, :] = jnp.dot(lhs, weights_ref[i, 0:3].reshape(768, 128), preferred_element_type=F32)


def far_kernel(acc_ref, from_ref, g17_ref, g16_ref, ang_ref, keep_ref, got_ref, weights_ref,
               out_ref, rows, cart, wind):
    blocks, piece = weights_ref.shape[0], wind.shape[0]
    from17 = from_ref[...] > 1.5
    from16 = (from_ref[...] > 0.5) & ~from17
    for c in range(3):
        for h in range(2):
            at = slice(blocks * (2 * c + h), blocks * (2 * c + h + 1))
            rows[h, pl.ds(c, blocks, stride=3), :] = jnp.where(
                from16, g16_ref[at, :].astype(F32), jnp.where(from17, g17_ref[at, :].astype(F32), 0.0)
            )
    for i in range(blocks):
        at = slice(3 * i, 3 * i + 3)
        cart[at, :] = acc_ref[at, :] + jnp.dot(
            jnp.concatenate([rows[0, at, :], rows[1, at, :]], axis=1).astype(BF16),
            weights_ref[i, 3],
            preferred_element_type=F32,
        )
    x, y, z = (cart[pl.ds(c, blocks, stride=3), :] for c in range(3))
    first = lax.axis_index("mem") * piece
    sa, ca = sin_cos(ang_ref[pl.ds(first, blocks, stride=2), :])
    sp, cp = sin_cos(ang_ref[pl.ds(first + 1, blocks, stride=2), :])
    wind[pl.ds(0, blocks, stride=2), :] = -sa * x + ca * y
    wind[pl.ds(1, blocks, stride=2), :] = -sp * ca * x - sp * sa * y + cp * z
    total = keep_ref[...] + got_ref[...]
    for n in range(out_ref.shape[0]):
        out_ref[n, 0:piece, :] = wind[...]
        out_ref[n, piece:, :] = total


def out_kernel(members_ref, all_ref, out_ref, delta, buffer, sems):
    piece = delta.shape[0] // all_ref.shape[0]
    for h in range(2):
        for b in range(2):
            mean = (all_ref[4 * h + b, piece:, :] + all_ref[4 * h + b + 2, piece:, :]) / F32(80.0)
            first = 4 * h + 2 * b
            for n in range(2):
                at = slice((first + n) * piece, (first + n + 1) * piece)
                delta[at, :] = all_ref[first + n, 0:piece, :] - mean[n * piece : (n + 1) * piece, :]
    groups = sems.shape[0]
    each = members_ref.shape[0] // groups
    copies = [
        pltpu.make_async_copy(buffer.at[pl.ds(each * n, each)], out_ref.at[pl.ds(each * n, each)], sems.at[n])
        for n in range(groups)
    ]
    for n in range(groups):
        for i in range(each * n, each * (n + 1)):
            buffer[i] = members_ref[i] + delta[...]
        copies[n].start()
    for copy in copies:
        copy.wait()


def call(kernel, name, outs, specs, scratch=(), out_space=pltpu.VMEM, cost=1.0):
    shapes = tuple(out_space(shape, dtype) for shape, dtype in outs)
    out_specs = tuple(pl.BlockSpec(memory_space=out_space) for _ in outs)

    def run(*args):
        args = [placed(x, spec) for x, spec in zip(args, specs, strict=True)]
        return pl.pallas_call(
            kernel, out_shape=shapes, in_specs=specs, out_specs=out_specs, scratch_shapes=list(scratch), name=name,
            cost_estimate=pl.CostEstimate(flops=int(cost * 1e9), bytes_accessed=int(cost * 3.6e6), transcendentals=0),
            compiler_params=pltpu.CompilerParams(vmem_limit_bytes=8 * 2**20),
        )(*args)

    return run


def shards(members, increment, fine_angles, coarse_angles, remap_weights, sources, counts):
    mems, tiles = lax.axis_size("mem"), lax.axis_size("tile")
    weights = remap_weights[0]
    blocks = weights.shape[0]
    ids = sources[0].T
    flip = mems // 2
    far = tiles // 2

    def send(x, mem_flip, tile_shift):
        pairs = [
            (a * tiles + b, (a ^ mem_flip) * tiles + (b + tile_shift) % tiles)
            for a in range(mems)
            for b in range(tiles)
        ]
        return lax.ppermute(x, ("mem", "tile"), pairs)

    def shifted(shift):
        pairs = []
        for a in range(mems):
            for b in range(tiles):
                c = (b + shift) % tiles
                near = a ^ flip if b // far != c // far else a
                pairs.append((a * tiles + b, near * tiles + c))
        return pairs

    axes = ("mem", "tile")
    p17, p16 = shifted(far + 1), shifted(far)
    r17, r16 = (lax.ppermute(ids, axes, p) for p in (p17, p16))

    inc_rows, ang_rows, members_rows = flat(increment), flat(fine_angles), flat(members)
    fine_rows = inc_rows.shape[0]
    count, total_rows = members_rows.shape[:2]
    piece = total_rows // mems
    row = lambda n, dtype=F32: ((n, 128), dtype)
    whole = (3, fine_rows // 2, 128)
    even, members_rows, mine, other = call(
        first_kernel,
        "fine_cart",
        [(whole, BF16), (members_rows.shape, F32)] + [row(4 * piece)] * 2,
        [HBM] * 3,
        [pltpu.VMEM(inc_rows.shape, F32)] * 2
        + [pltpu.VMEM((3, fine_rows, 128), F32), pltpu.SemaphoreType.DMA((4, 2)), pltpu.SemaphoreType.DMA((1,))],
        cost=20,
    )(inc_rows, ang_rows, members_rows)

    below = lax.ppermute(even, axes, shifted(1))

    got = send(other, flip, 0)

    rows = (6 * blocks, 128)
    s17, s16 = call(pick_kernel, "pick_rows", [(rows, BF16), (rows, BF16)], [VMEM] * 3, cost=20)(r17, r16, even)
    g17, g16 = (lax.ppermute(x, axes, [(d, a) for a, d in p]) for x, p in ((s17, p17), (s16, p16)))

    keep, other = call(pair_kernel, "pair_sum", [row(2 * piece)] * 2, [VMEM, VMEM, ANY])(mine, got, s16)
    got = send(other, 1, 0)

    near = call(
        near_kernel,
        "near_slots",
        [row(3 * blocks), row(blocks)],
        [VMEM] * 5,
        [pltpu.VMEM((6, 3 * blocks, 128), F32), pltpu.VMEM((3, 4 * blocks, 128), F32)],
        cost=20,
    )(ids, counts, even, below, weights)

    (payload,) = call(
        far_kernel,
        "far_slots",
        [((mems, 3 * piece, 128), F32)],
        [VMEM] * 8,
        [pltpu.VMEM((2, 3 * blocks, 128), F32), pltpu.VMEM((3 * blocks, 128), F32), pltpu.VMEM((piece, 128), F32)],
    )(*near, g17, g16, flat(coarse_angles), keep, got, weights)
    payload = lax.all_to_all(payload, "mem", 0, 0, tiled=True)
    (out,) = call(
        out_kernel,
        "recentre",
        [(members_rows.shape, F32)],
        [VMEM, VMEM],
        [pltpu.VMEM((total_rows, 128), F32), pltpu.VMEM(members_rows.shape, F32), pltpu.SemaphoreType.DMA((1,))],
        pltpu.HBM,
    )(members_rows, payload)
    return unflat(out)


def solution(mesh):
    in_specs = (
        P("mem", None, "tile"),
        P(None, "tile"),
        P(None, "tile"),
        P(None, "tile"),
        P("tile", "mem", None, None, None),
        P("tile", "mem", None),
        P("tile", "mem"),
    )
    out_specs = P("mem", None, "tile")
    return jax.shard_map(shards, mesh=mesh, in_specs=in_specs, out_specs=out_specs, check_vma=False)
```
